512 devices in a mesh: expert: 128 (over z, y, core), dp: 4 (over x).
Axes of the slice: x: 4, y: 4, z: 16, core: 2. Of those that a mesh axis runs over, the one named last changes fastest.
Arguments:
- tokens: bfloat16 [65536, 2048], P(('expert', 'dp')), may hold values from -6 to 6
- norm_gain: float32 [2048], replicated, may hold values from 0.25 to 1.75
- routing: int32 [65536, 2], P(('expert', 'dp')), may hold values from 0 to 127, as said below
- gate_scores: float32 [65536, 2], P(('expert', 'dp')), may hold values from 0.05 to 1
- w_gate: bfloat16 [128, 2048, 1024], P('expert', None, 'dp'), may hold values from -0.125 to 0.125
- w_up: bfloat16 [128, 2048, 1024], P('expert', None, 'dp'), may hold values from -0.125 to 0.125
- w_down: bfloat16 [128, 1024, 2048], P('expert', None, 'dp'), may hold values from -0.1875 to 0.1875
Outputs:
- combined: bfloat16 [65536, 2048], P(('expert', 'dp'))
The draws below stay inside these ranges and needn't reach their ends.
Inputs may be any that keep to these rules, and one draw needn't show every extreme that they name: `routing`: each row names 2 different experts. Two experts, the same on every device, are each named by exactly 4 of the 128 rows of every device; every other expert is named by at most 2 rows of one device, and some reach 2.
All inputs are finite; a program needn't handle non-finite values.
Results may differ from the reference program's by a relative error of at most 0.007.
Values may be sent and summed in bfloat16 or wider, within the bound.
No kernel may reach another device: no remote copies, remote signals or barrier semaphores. Data moves between devices by JAX's collectives and lax.ppermute only.
A program may use at most 128 MiB of HBM per device.

```python
import math
import jax
import jax.numpy as jnp
from jax import lax

D = 2048
FF = 1024
TOK_DEV = 128
EXPERTS = 128
TOP = 2
CAP = 4
KCAP = 2
SLOTS = 4
TOKENS = 65536
N_EXPERT = 128
N_DP = 4


def draw_routing(key, part):
    block_count = N_EXPERT * N_DP
    others_count = EXPERTS - 2
    key_order, key_rest = jax.random.split(key)
    order = jax.random.permutation(key_order, EXPERTS).astype(jnp.int32)
    hot_pair = order[:2]
    others = order[2:]

    def one_block(block_key):
        key_one, key_two, key_three, key_four = jax.random.split(block_key, 4)
        has_first = (jax.random.permutation(key_one, TOK_DEV) < CAP).astype(jnp.int32)
        has_second = (jax.random.permutation(key_two, TOK_DEV) < CAP).astype(jnp.int32)
        shuffled = jax.random.permutation(key_three, others)
        offset = jax.random.randint(key_four, (), 0, others_count)
        hot_count = has_first + has_second
        needed = TOP - hot_count
        begins = jnp.cumsum(needed) - needed
        column = jnp.arange(TOP, dtype=jnp.int32)[None, :]
        position = (begins[:, None] + column - hot_count[:, None] + offset) % others_count
        picked = shuffled[position]
        lead_hot = jnp.where(has_first[:, None] == 1, hot_pair[0], hot_pair[1])
        hot_column = jnp.where(column == 0, lead_hot, hot_pair[1])
        return jnp.where(column < hot_count[:, None], hot_column, picked)
    block_keys = jax.random.split(key_rest, block_count)
    return jax.vmap(one_block)(block_keys).reshape(block_count * TOK_DEV, TOP).astype(jnp.int32)


def level_of(rng, shape, cuts, low, largest):
    factor_of, own = 1.0, jax.random.fold_in(rng, 6)
    for axis_at, shards_of in cuts:
        draws = jnp.exp(jax.random.uniform(jax.random.fold_in(own, axis_at), (shards_of,), jnp.float32, low / len(cuts), largest / len(cuts)))
        factor_of = factor_of * jnp.repeat(draws, shape[axis_at] // shards_of).reshape([-1 if axis == axis_at else 1 for axis in range(len(shape))])
    return factor_of


def normal_values(rng, dims, scale, most, pieces=(), kind=jnp.bfloat16):
    result = jax.random.normal(rng, dims, jnp.float32) * scale
    if len(pieces) > 0:
        result = level_of(rng, dims, pieces, -0.22, 0.18) * result
    return jnp.clip(result, min=-most, max=most).astype(kind)


def setup_inputs(seed: int = 0) -> dict:
    arg_keys = jax.random.split(jax.random.key(seed), 8)
    return {
        "tokens": normal_values(arg_keys[0], (TOKENS, D), 1.0, 6.0, ((0, 512),)),
        "norm_gain": jnp.clip(1.0 + 0.15 * jax.random.normal(arg_keys[1], (D,), jnp.float32), 0.25, 1.75),
        "routing": draw_routing(jax.random.fold_in(arg_keys[7], 71), 0),
        "gate_scores": jnp.clip(jnp.exp(math.log(1.0) - 2.9957323 * jax.random.uniform(arg_keys[3], (TOKENS, TOP), jnp.float32) ** level_of(arg_keys[3], (TOKENS, TOP), ((0, 512),), -0.2, 0.2)), 0.05, 1.0),
        "w_gate": normal_values(arg_keys[4], (EXPERTS, D, FF), D ** -0.5, 0.125, ((0, 128), (2, 4))),
        "w_up": normal_values(arg_keys[5], (EXPERTS, D, FF), D ** -0.5, 0.125, ((0, 128), (2, 4))),
        "w_down": normal_values(arg_keys[6], (EXPERTS, FF, D), FF ** -0.5, 0.1875, ((0, 128), (2, 4))),
    }


def reference(tokens, norm_gain, routing, gate_scores, w_gate, w_up, w_down):
    as_float = tokens.astype(jnp.float32)
    scale_rms = lax.rsqrt(lax.optimization_barrier(jnp.mean(as_float * as_float, axis=1, keepdims=True)) + 1e-06)
    normed = (as_float * scale_rms * norm_gain).astype(jnp.bfloat16)
    weights = gate_scores / lax.optimization_barrier(jnp.sum(gate_scores, axis=1, keepdims=True))
    flat_ids = routing.reshape(-1)
    flat_weight = weights.reshape(-1)
    experts = w_gate.shape[0]
    expert_range = jnp.arange(experts, dtype=jnp.int32)
    load_count = lax.optimization_barrier(jnp.sum((flat_ids[:, None] == expert_range[None, :]).astype(jnp.int32), axis=0))
    hottest = jnp.argmax(load_count).astype(jnp.int32)
    runner_up = jnp.argmax(jnp.where(expert_range == hottest, -1, load_count)).astype(jnp.int32)
    device_count = N_EXPERT * N_DP

    def run_expert(running, expert_id, row_bound, skipped):
        live_mask = (flat_ids == expert_id) & jnp.logical_not(skipped)
        pair_index = jnp.nonzero(live_mask, size=row_bound, fill_value=0)[0]
        valid = jnp.arange(row_bound) < jnp.sum(live_mask.astype(jnp.int32))
        token_of = pair_index // TOP
        picked = normed[token_of]
        gate_part = jnp.dot(picked, w_gate[expert_id], preferred_element_type=jnp.float32)
        up_part = jnp.dot(picked, w_up[expert_id], preferred_element_type=jnp.float32)
        hidden = (jax.nn.silu(gate_part) * up_part).astype(jnp.bfloat16)
        expert_out = jnp.dot(hidden, w_down[expert_id], preferred_element_type=jnp.float32).astype(jnp.bfloat16)
        scaled = expert_out.astype(jnp.float32) * jnp.where(valid, flat_weight[pair_index], 0.0)[:, None]
        return running.at[token_of].add(scaled)

    def scan_step(running, expert_id):
        skipped = (expert_id == hottest) | (expert_id == runner_up)
        return (run_expert(running, expert_id, KCAP * device_count, skipped), None)
    running = jnp.zeros((tokens.shape[0], tokens.shape[1]), jnp.float32)
    running, _ = lax.scan(scan_step, running, expert_range)
    never = jnp.zeros((), dtype=bool)
    for hot_id in (hottest, runner_up):
        running = run_expert(running, hot_id, SLOTS * device_count, never)
    return running.astype(jnp.bfloat16)
```

```python
import jax
import jax.numpy as jnp
from jax import lax
from jax.experimental import pallas as pl
from jax.experimental.pallas import tpu as pltpu
from jax.sharding import Mesh, PartitionSpec as P

E_AXES = ("z", "y", "c")
SLOT = 2
VMEM = pl.BlockSpec(memory_space=pltpu.VMEM)


def first_kernel(tok_ref, gain_ref, rt_ref, main_ref, ext_ref, tgt_ref, hot_ref):
    toks, experts = tok_ref.shape[0], main_ref.shape[0] // SLOT
    x = tok_ref[...].astype(jnp.float32)
    scale = lax.rsqrt(jnp.mean(x * x, axis=1, keepdims=True) + 1e-06)
    normed = (x * scale * gain_ref[...]).astype(jnp.bfloat16)
    lane = lax.broadcasted_iota(jnp.int32, (toks, experts), 1)
    ids = [rt_ref[:, k : k + 1] for k in range(2)]
    hots = [i == lane for i in ids]
    both = (hots[0] | hots[1]).astype(jnp.float32)
    row = lax.broadcasted_iota(jnp.int32, (toks, toks), 0)
    col = lax.broadcasted_iota(jnp.int32, (toks, toks), 1)
    before = (row > col).astype(jnp.bfloat16)
    count = jnp.dot(before, both.astype(jnp.bfloat16), preferred_element_type=jnp.float32)
    busy = jnp.sum(both, axis=0, keepdims=True) > SLOT + 0.5
    eid = lax.broadcasted_iota(jnp.int32, (1, experts), 1)
    low = jnp.min(jnp.where(busy, eid, experts - 1), axis=1, keepdims=True)
    high = jnp.max(jnp.where(busy, eid, 0), axis=1, keepdims=True)
    targets = []
    for k in range(2):
        rank = jnp.sum(jnp.where(hots[k], count, 0.0), axis=1, keepdims=True).astype(jnp.int32)
        over = experts * SLOT + jnp.where(ids[k] == high, 2, 0) + rank - SLOT
        targets.append(jnp.where(rank < SLOT, ids[k] * SLOT + rank, over))
        tgt_ref[:, k : k + 1] = targets[k]
    for ref, base in ((main_ref, 0), (ext_ref, experts * SLOT)):
        slots = max(ref.shape[0], 128)
        slot = lax.broadcasted_iota(jnp.int32, (toks, slots), 1) + base
        pick = ((slot == targets[0]) | (slot == targets[1])).astype(jnp.float32)
        rows = jnp.dot(
            pick.T.astype(jnp.bfloat16), normed, preferred_element_type=jnp.float32
        ).astype(jnp.bfloat16)
        ref[...] = rows[: ref.shape[0]]
    hot_ref[:, 0:1] = low
    hot_ref[:, 1:2] = high


def last_kernel(res_ref, ext_ref, tgt_ref, gs_ref, out_ref):
    toks, slots = out_ref.shape[0], res_ref.shape[0]
    weights = gs_ref[...] / jnp.sum(gs_ref[...], axis=1, keepdims=True)
    total = None
    for ref, base in ((res_ref, 0), (ext_ref, slots)):
        slot = lax.broadcasted_iota(jnp.int32, (toks, ref.shape[0]), 1) + base
        mix = sum(jnp.where(slot == tgt_ref[:, k : k + 1], weights[:, k : k + 1], 0.0) for k in range(2))
        coarse = mix.astype(jnp.bfloat16)
        fine = (mix - coarse.astype(jnp.float32)).astype(jnp.bfloat16)
        for part in (fine, coarse):
            term = jnp.dot(part, ref[...], preferred_element_type=jnp.float32)
            total = term if total is None else total + term
    out_ref[...] = total.astype(jnp.bfloat16)


def flip(n, bit):
    return [(i, i ^ bit) for i in range(n)]


def ring(n, k):
    return [(i, (i + k) % n) for i in range(n)]


def gather_ring(x):
    half = x.shape[0] // 2
    ahead = lax.ppermute(x, "dp", ring(4, -1))
    behind = lax.ppermute(x, "dp", ring(4, 1))
    far_a = lax.ppermute(ahead[:half], "dp", ring(4, -1))
    far_b = lax.ppermute(behind[half:], "dp", ring(4, 1))
    return [x, ahead, jnp.concatenate([far_a, far_b], 0), behind]


def steps_of(mesh):
    steps = []
    for axis in ("z", "y", "c"):
        bit = mesh.shape[axis] // 2
        while bit:
            steps.append((axis, bit))
            bit //= 2
    return steps


def body(mesh, tokens, norm_gain, routing, gate_scores, w_gate, w_up, w_down):
    toks, width = tokens.shape
    experts = 1
    for axis in E_AXES:
        experts *= mesh.shape[axis]
    bf16, f32, i32 = jnp.bfloat16, jnp.float32, jnp.int32
    main, extra, target, hot = pl.pallas_call(
        first_kernel,
        out_shape=[
            jax.ShapeDtypeStruct((experts * SLOT, width), bf16),
            jax.ShapeDtypeStruct((16, width), bf16),
            jax.ShapeDtypeStruct((toks, 2), i32),
            jax.ShapeDtypeStruct((1, 2), i32),
        ],
        in_specs=[VMEM] * 3,
        out_specs=[VMEM] * 4,
        compiler_params=pltpu.CompilerParams(vmem_limit_bytes=40 * 1024 * 1024),
    )(tokens, norm_gain.reshape(1, width), routing)

    gate_all = lax.all_gather(w_gate[0], "dp", axis=0, tiled=False)
    up_all = lax.all_gather(w_up[0], "dp", axis=0, tiled=False)
    down = gather_ring(w_down[0])

    got = lax.all_to_all(main.reshape(experts, SLOT, width), E_AXES, 0, 0, tiled=True)
    steps = steps_of(mesh)
    held = extra[:4].reshape(1, 4 * width)
    for axis, bit in steps:
        held = jnp.concatenate([held, lax.ppermute(held, axis, flip(mesh.shape[axis], bit))], 0)
    place = [lax.axis_index(a) for a in E_AXES]
    me = (place[0] * mesh.shape["y"] + place[1]) * mesh.shape["c"] + place[2]
    low, high = hot[0, 0], hot[0, 1]
    mine = jnp.where(me == low, held[:, : 2 * width], held[:, 2 * width :])
    rows = jnp.concatenate([got.reshape(experts * SLOT, width), mine[:, :width], mine[:, width:]], 0)

    hidden = []
    for q in range(4):
        g = jnp.dot(rows, gate_all[q], preferred_element_type=f32)
        u = jnp.dot(rows, up_all[q], preferred_element_type=f32)
        hidden.append((jax.nn.silu(g) * u).astype(bf16))
    hidden = jnp.concatenate(hidden, 1)
    parts = [jnp.dot(hidden, d, preferred_element_type=f32).astype(bf16) for d in down]
    at = lax.axis_index("dp")
    cols = w_down.shape[2]
    ordered = jnp.zeros((rows.shape[0], width), bf16)
    for k in range(4):
        ordered = lax.dynamic_update_slice(ordered, parts[k], (0, lax.rem(at + k, 4) * cols))
    done = ordered[: experts * SLOT].reshape(experts, SLOT, width)
    back = lax.all_to_all(done, E_AXES, 0, 0, tiled=True).reshape(experts * SLOT, width)

    over = ordered[experts * SLOT :].reshape(2, experts, width)
    over = jnp.concatenate([over[0], over[1]], 1)
    over = jnp.concatenate([over, over], 1)
    away = [me ^ low, me ^ high]
    left = (1 << len(steps)) - 1
    bits = {}
    weight = {"c": 1, "y": mesh.shape["c"], "z": mesh.shape["c"] * mesh.shape["y"]}
    for axis, bit in reversed(steps):
        half = over.shape[0] // 2
        sent = lax.ppermute(over[half:], axis, flip(mesh.shape[axis], bit))
        keep = [(a & left) == 0 for a in away]
        pick = jnp.where(jnp.arange(4 * width)[None, :] < 2 * width, keep[0], keep[1])
        over = jnp.where(pick, over[:half], sent)
        left -= weight[axis] * bit
    over = over.reshape(4, width)

    return pl.pallas_call(
        last_kernel,
        out_shape=jax.ShapeDtypeStruct((toks, width), bf16),
        in_specs=[VMEM] * 4,
        out_specs=VMEM,
        compiler_params=pltpu.CompilerParams(vmem_limit_bytes=40 * 1024 * 1024),
    )(back, jnp.pad(over, ((0, 124), (0, 0))), target, gate_scores)


def solution(mesh):
    fine = Mesh(mesh.devices.reshape(16, 4, 2, 4), ("z", "y", "c", "dp"))
    rows = P((*E_AXES, "dp"), None)
    weights = P(E_AXES, None, "dp")
    return jax.shard_map(
        lambda *args: body(fine, *args),
        mesh=fine,
        in_specs=(rows, P(), rows, rows, weights, weights, weights),
        out_specs=rows,
        check_vma=False,
    )
```

```python
import jax
import jax.numpy as jnp
from jax import lax
from jax.experimental import pallas as pl
from jax.experimental.pallas import tpu as pltpu
from jax.sharding import Mesh, PartitionSpec as P

E_AXES = ("z", "y", "c")
PLANE = ("y", "c")
SLOT = 2
VMEM = pl.BlockSpec(memory_space=pltpu.VMEM)
SMEM = pl.BlockSpec(memory_space=pltpu.SMEM)


def matmul(a, b):
    return jnp.dot(a, b, preferred_element_type=jnp.float32)


def iota(shape, dim):
    return lax.broadcasted_iota(jnp.int32, shape, dim)


def first_kernel(plane, tok_ref, gain_ref, rt_ref, out_ref, tgt_ref, hot_ref):
    toks, width = tok_ref.shape
    slots = out_ref.shape[0]
    experts, piece = slots // SLOT, width // plane
    x = tok_ref[...].astype(jnp.float32)
    scale = lax.rsqrt(jnp.mean(x * x, axis=1, keepdims=True) + 1e-06)
    normed = (x * scale * gain_ref[...]).astype(jnp.bfloat16)
    lane = iota((toks, experts), 1)
    ids = [rt_ref[:, k : k + 1] for k in range(2)]
    hots = [i == lane for i in ids]
    both = (hots[0] | hots[1]).astype(jnp.float32)
    before = (iota((toks, toks), 0) > iota((toks, toks), 1)).astype(jnp.bfloat16)
    count = matmul(before, both.astype(jnp.bfloat16))
    busy = jnp.sum(both, axis=0, keepdims=True) > SLOT + 0.5
    eid = iota((1, experts), 1)
    low = jnp.min(jnp.where(busy, eid, experts - 1), axis=1, keepdims=True)
    high = jnp.max(jnp.where(busy, eid, 0), axis=1, keepdims=True)
    targets = []
    for k in range(2):
        rank = jnp.sum(jnp.where(hots[k], count, 0.0), axis=1, keepdims=True).astype(jnp.int32)
        over = slots + jnp.where(ids[k] == high, SLOT, 0) + rank - SLOT
        targets.append(jnp.where(rank < SLOT, ids[k] * SLOT + rank, over))
        tgt_ref[:, k : k + 1] = targets[k]
    slot = iota((toks, slots), 1)

    def pick(wanted):
        chosen = ((wanted == targets[0]) | (wanted == targets[1])).astype(jnp.float32)
        return chosen.T.astype(jnp.bfloat16)

    out_ref[:, :width] = matmul(pick(slot), normed).astype(jnp.bfloat16)
    owner = (iota((slots, toks), 0) // SLOT) % plane
    for h in range(2):
        chosen = pick(slots + h * SLOT + slot % SLOT)
        total = jnp.zeros((slots, piece), jnp.float32)
        for j in range(plane):
            part = matmul(chosen, normed[:, j * piece : (j + 1) * piece])
            total = jnp.where(owner[:, :1] == j, part, total)
        out_ref[:, width + h * piece : width + (h + 1) * piece] = total.astype(jnp.bfloat16)
    hot_ref[:, 0:1] = low
    hot_ref[:, 1:2] = high


def last_kernel(plane, hot_ref, res_ref, tgt_ref, gs_ref, out_ref):
    toks, width = out_ref.shape
    slots, piece = res_ref.shape[0], width // plane
    weights = gs_ref[...] / jnp.sum(gs_ref[...], axis=1, keepdims=True)

    def mix(wanted, alive=True):
        hits = [(wanted == tgt_ref[:, k : k + 1]) & alive for k in range(2)]
        exact = sum(jnp.where(hits[k], weights[:, k : k + 1], 0.0) for k in range(2))
        coarse = exact.astype(jnp.bfloat16)
        return (exact - coarse.astype(jnp.float32)).astype(jnp.bfloat16), coarse

    usual = mix(iota((toks, slots), 1))
    spot = iota((toks, plane * SLOT), 1)
    over = []
    for h in range(2):
        start = pl.multiple_of(hot_ref[h] // plane * (plane * SLOT), plane * SLOT)
        over.append(res_ref[pl.ds(start, plane * SLOT), width + h * piece : width + (h + 1) * piece])
    for j in range(plane):
        cols = slice(j * piece, (j + 1) * piece)
        total = sum(matmul(p, res_ref[:, cols]) for p in usual)
        for h in range(2):
            parts = mix(slots + h * SLOT + spot % SLOT, spot // SLOT == j)
            total += sum(matmul(p, over[h]) for p in parts)
        out_ref[:, cols] = total.astype(jnp.bfloat16)


def hidden_of(rows, both_ref, hid_ref):
    for q in range(both_ref.shape[0]):
        cols = both_ref.shape[2] // 2
        g, u = matmul(rows, both_ref[q, :, :cols]), matmul(rows, both_ref[q, :, cols:])
        hid_ref[:, q * cols : (q + 1) * cols] = (jax.nn.silu(g) * u).astype(jnp.bfloat16)


def results(hidden, down, at):
    own, ahead, far_a, far_b, behind = down
    half = far_a.shape[0]
    yield at, matmul(hidden, own[...])
    yield lax.rem(at + 1, 4), matmul(hidden, ahead[...])
    yield lax.rem(at + 2, 4), matmul(hidden[:, :half], far_a[...]) + matmul(hidden[:, half:], far_b[...])
    yield lax.rem(at + 3, 4), matmul(hidden, behind[...])


def main_kernel(at_ref, rows_ref, both_ref, *refs):
    down, out_ref, hid_ref = refs[:5], *refs[5:]
    hidden_of(rows_ref[:, : both_ref.shape[1]], both_ref, hid_ref)
    for index, value in results(hid_ref[...], down, at_ref[0]):
        cols = value.shape[1]
        out_ref[:, pl.ds(pl.multiple_of(index * cols, cols), cols)] = value.astype(jnp.bfloat16)


def extra_kernel(at_ref, rows_ref, both_ref, *refs):
    down, out_ref, row_ref, hid_ref = refs[:5], *refs[5:]
    pieces, _, piece = rows_ref.shape
    for j in range(pieces):
        row_ref[:, j * piece : (j + 1) * piece] = rows_ref[j]
    hidden_of(row_ref[...], both_ref, hid_ref)
    for index, value in results(hid_ref[...], down, at_ref[0]):
        parts = value.shape[1] // piece
        for i in range(parts):
            out_ref[index * parts + i] = value[:, i * piece : (i + 1) * piece].astype(jnp.bfloat16)


def ring(n, k):
    return [(i, (i + k) % n) for i in range(n)]


def gather_ring(x):
    half = x.shape[0] // 2
    ahead, behind = lax.ppermute(x, "dp", ring(4, -1)), lax.ppermute(x, "dp", ring(4, 1))
    far_a = lax.ppermute(ahead[:half], "dp", ring(4, -1))
    far_b = lax.ppermute(behind[half:], "dp", ring(4, 1))
    return x, ahead, far_a, far_b, behind


def call(kernel, out, *args, scalars=0, scratch=()):
    return pl.pallas_call(
        kernel,
        out_shape=out,
        in_specs=[SMEM] * scalars + [VMEM] * (len(args) - scalars),
        out_specs=jax.tree.map(lambda _: VMEM, out),
        scratch_shapes=list(scratch),
        compiler_params=pltpu.CompilerParams(vmem_limit_bytes=44 * 1024 * 1024),
    )(*args)


def body(mesh, tokens, norm_gain, routing, gate_scores, w_gate, w_up, w_down):
    toks, width = tokens.shape
    plane = mesh.shape["y"] * mesh.shape["c"]
    experts = mesh.shape["z"] * plane
    slots, piece = experts * SLOT, width // plane
    bf16, i32, shape = jnp.bfloat16, jnp.int32, jax.ShapeDtypeStruct
    units = w_gate.shape[2] * 4

    both = lax.all_gather(jnp.concatenate([w_gate[0], w_up[0]], 1), "dp", axis=0, tiled=False)
    down = gather_ring(w_down[0])
    sent, target, hot = call(
        lambda *refs: first_kernel(plane, *refs),
        [shape((slots, width + 2 * piece), bf16), shape((toks, 2), i32), shape((1, 2), i32)],
        tokens,
        norm_gain.reshape(1, width),
        routing,
    )
    trade = lambda x: lax.all_to_all(
        x.reshape(experts, SLOT, x.shape[1]), E_AXES, 0, 0, tiled=True
    ).reshape(x.shape)
    at = lax.axis_index("dp").reshape(1)
    z = lax.axis_index("z")
    hot = hot.reshape(2)
    low, high = hot[0], hot[1]

    got = trade(sent)
    to_low = (jnp.arange(plane) == low % plane) & (z == low // plane)
    packed = jnp.where(
        to_low[:, None, None], got[None, :, width : width + piece], got[None, :, width + piece :]
    )
    pieces = lax.all_to_all(packed, PLANE, 0, 0, tiled=True)
    hid = pltpu.VMEM((slots, units), bf16)
    over = call(
        extra_kernel,
        shape((plane, slots, piece), bf16),
        at, pieces, both, *down,
        scalars=1,
        scratch=[pltpu.VMEM((slots, width), bf16), hid],
    )
    over = lax.all_to_all(over, PLANE, 0, 0, tiled=True)
    done = call(main_kernel, shape((slots, width), bf16), at, got, both, *down, scalars=1, scratch=[hid])
    take = lambda h: lax.dynamic_index_in_dim(over, h % plane, 0, keepdims=False)
    back = trade(jnp.concatenate([done, take(low), take(high)], 1))
    return call(
        lambda *refs: last_kernel(plane, *refs),
        shape((toks, width), bf16),
        hot, back, target, gate_scores,
        scalars=1,
    )


def solution(mesh):
    fine = Mesh(mesh.devices.reshape(16, 4, 2, 4), ("z", "y", "c", "dp"))
    rows = P((*E_AXES, "dp"), None)
    weights = P(E_AXES, None, "dp")
    return jax.shard_map(
        lambda *args: body(fine, *args),
        mesh=fine,
        in_specs=(rows, P(), rows, rows, weights, weights, weights),
        out_specs=rows,
        check_vma=False,
    )
```

```python
import jax
import jax.numpy as jnp
from jax import lax
from jax.experimental import pallas as pl
from jax.experimental.pallas import tpu as pltpu
from jax.sharding import Mesh, PartitionSpec as P

E_AXES = ("z", "y", "c")
PLANE = ("y", "c")
SLOT = 2
VMEM = pl.BlockSpec(memory_space=pltpu.VMEM)
SMEM = pl.BlockSpec(memory_space=pltpu.SMEM)


def matmul(a, b):
    return jnp.dot(a, b, preferred_element_type=jnp.float32)


def iota(shape, dim):
    return lax.broadcasted_iota(jnp.int32, shape, dim)


def first_kernel(plane, tok_ref, gain_ref, rt_ref, out_ref, tgt_ref, hot_ref):
    toks, width = tok_ref.shape
    slots = out_ref.shape[0]
    experts, piece = slots // SLOT, width // plane
    x = tok_ref[...].astype(jnp.float32)
    scale = lax.rsqrt(jnp.mean(x * x, axis=1, keepdims=True) + 1e-06)
    normed = (x * scale * gain_ref[...]).astype(jnp.bfloat16)
    lane = iota((toks, experts), 1)
    ids = [rt_ref[:, k : k + 1] for k in range(2)]
    hots = [i == lane for i in ids]
    both = (hots[0] | hots[1]).astype(jnp.float32)
    before = (iota((toks, toks), 0) > iota((toks, toks), 1)).astype(jnp.bfloat16)
    count = matmul(before, both.astype(jnp.bfloat16))
    busy = jnp.sum(both, axis=0, keepdims=True) > SLOT + 0.5
    eid = iota((1, experts), 1)
    low = jnp.min(jnp.where(busy, eid, experts - 1), axis=1, keepdims=True)
    high = jnp.max(jnp.where(busy, eid, 0), axis=1, keepdims=True)
    targets = []
    for k in range(2):
        rank = jnp.sum(jnp.where(hots[k], count, 0.0), axis=1, keepdims=True).astype(jnp.int32)
        over = slots + jnp.where(ids[k] == high, SLOT, 0) + rank - SLOT
        targets.append(jnp.where(rank < SLOT, ids[k] * SLOT + rank, over))
        tgt_ref[:, k : k + 1] = targets[k]
    slot = iota((toks, slots), 1)

    def pick(wanted):
        chosen = ((wanted == targets[0]) | (wanted == targets[1])).astype(jnp.float32)
        return chosen.T.astype(jnp.bfloat16)

    out_ref[:, :width] = matmul(pick(slot), normed).astype(jnp.bfloat16)
    owner = (iota((slots, toks), 0) // SLOT) % plane
    for h in range(2):
        chosen = pick(slots + h * SLOT + slot % SLOT)
        total = jnp.zeros((slots, piece), jnp.float32)
        for j in range(plane):
            part = matmul(chosen, normed[:, j * piece : (j + 1) * piece])
            total = jnp.where(owner[:, :1] == j, part, total)
        out_ref[:, width + h * piece : width + (h + 1) * piece] = total.astype(jnp.bfloat16)
    hot_ref[:, 0:1] = low
    hot_ref[:, 1:2] = high


def last_kernel(plane, hot_ref, res_ref, more_ref, tgt_ref, gs_ref, out_ref):
    toks, width = out_ref.shape
    slots, piece, near = res_ref.shape[0], width // plane, res_ref.shape[1]
    weights = gs_ref[...] / jnp.sum(gs_ref[...], axis=1, keepdims=True)

    def mix(wanted, alive=True):
        hits = [(wanted == tgt_ref[:, k : k + 1]) & alive for k in range(2)]
        exact = sum(jnp.where(hits[k], weights[:, k : k + 1], 0.0) for k in range(2))
        coarse = exact.astype(jnp.bfloat16)
        return (exact - coarse.astype(jnp.float32)).astype(jnp.bfloat16), coarse

    usual = mix(iota((toks, slots), 1))
    spot = iota((toks, plane * SLOT), 1)
    base = width - near
    over = []
    for h in range(2):
        start = pl.multiple_of(hot_ref[h] // plane * (plane * SLOT), plane * SLOT)
        over.append(more_ref[pl.ds(start, plane * SLOT), base + h * piece : base + (h + 1) * piece])
    for j in range(plane):
        start = j * piece
        rows = res_ref[:, start : start + piece] if start < near else (
            more_ref[:, start - near : start - near + piece]
        )
        total = sum(matmul(p, rows) for p in usual)
        for h in range(2):
            parts = mix(slots + h * SLOT + spot % SLOT, spot // SLOT == j)
            total += sum(matmul(p, over[h]) for p in parts)
        out_ref[:, start : start + piece] = total.astype(jnp.bfloat16)


def blocks_of(at, all_ref, own, ahead, far_a, far_b, behind):
    deep = all_ref.shape[1] * 2 // 3
    half = far_a.shape[0]
    for k, ref in enumerate((own, ahead, None, behind)):
        index = lax.rem(at + k, 4)
        if ref is None:
            up, right = [far_a, far_b.at[: deep - half]], [far_b.at[deep - half :]]
        else:
            up, right = [ref.at[:deep]], [ref.at[deep:]]
        yield index, [all_ref.at[index, :deep]], up, ([all_ref.at[index, deep:]], right)


def product(rows, parts):
    start, total = 0, None
    for ref in parts:
        term = matmul(rows[:, start : start + ref.shape[0]], ref[...])
        total = term if total is None else total + term
        start += ref.shape[0]
    return total


def expert(at, rows, weights, hid_ref, put):
    for index, gate, up, _ in blocks_of(at, *weights):
        g, u = product(rows, gate), product(rows, up)
        cols = g.shape[1]
        hid_ref[:, pl.ds(pl.multiple_of(index * cols, cols), cols)] = (jax.nn.silu(g) * u).astype(
            jnp.bfloat16
        )
    for index, _, _, down in blocks_of(at, *weights):
        for i, d in enumerate(down):
            put(index * 2 + i, product(hid_ref[...], d).astype(jnp.bfloat16))


def main_kernel(at_ref, rows_ref, *refs):
    weights, out_ref, hid_ref = refs[:6], *refs[6:]

    def put(index, value):
        cols = value.shape[1]
        out_ref[:, pl.ds(pl.multiple_of(index * cols, cols), cols)] = value

    expert(at_ref[0], rows_ref[:, : out_ref.shape[1]], weights, hid_ref, put)


def extra_kernel(at_ref, rows_ref, *refs):
    weights, out_ref, row_ref, hid_ref = refs[:6], *refs[6:]
    pieces, _, piece = rows_ref.shape
    for j in range(pieces):
        row_ref[:, j * piece : (j + 1) * piece] = rows_ref[j]

    def put(index, value):
        out_ref[index ^ at_ref[1]] = value

    expert(at_ref[0], row_ref[...], weights, hid_ref, put)


def ring(n, k):
    return [(i, (i + k) % n) for i in range(n)]


def pass_kernel(ahead_ref, behind_ref, a_ref, b_ref):
    half = a_ref.shape[0]
    a_ref[...] = ahead_ref[:half]
    b_ref[...] = behind_ref[half:]


def gather_ring(x):
    half = x.shape[0] // 2
    ahead, behind = lax.ppermute(x, "dp", ring(4, -1)), lax.ppermute(x, "dp", ring(4, 1))
    part = jax.ShapeDtypeStruct((half, x.shape[1]), x.dtype)
    a, b = call(pass_kernel, [part, part], ahead, behind, flops=40000000000)
    return x, ahead, a, b, behind


def pass_on(x, ahead, a, b, behind):
    return x, ahead, lax.ppermute(a, "dp", ring(4, -1)), lax.ppermute(b, "dp", ring(4, 1)), behind


def call(kernel, out, *args, scalars=0, scratch=(), flops=None):
    return pl.pallas_call(
        kernel,
        out_shape=out,
        in_specs=[SMEM] * scalars + [VMEM] * (len(args) - scalars),
        out_specs=jax.tree.map(lambda _: VMEM, out),
        scratch_shapes=list(scratch),
        compiler_params=pltpu.CompilerParams(vmem_limit_bytes=44 * 1024 * 1024),
        cost_estimate=None
        if flops is None
        else pl.CostEstimate(flops=flops, bytes_accessed=0, transcendentals=0),
    )(*args)


def body(mesh, tokens, norm_gain, routing, gate_scores, w_gate, w_up, w_down):
    toks, width = tokens.shape
    plane = mesh.shape["y"] * mesh.shape["c"]
    experts = mesh.shape["z"] * plane
    slots, piece = experts * SLOT, width // plane
    bf16, i32, shape = jnp.bfloat16, jnp.int32, jax.ShapeDtypeStruct
    units = w_gate.shape[2] * 4

    cols = w_down.shape[2] // 2
    gate = lax.all_gather(jnp.concatenate([w_gate[0], w_down[0, :, :cols]], 0), "dp", axis=0, tiled=False)
    packed = gather_ring(jnp.concatenate([w_up[0], w_down[0, :, cols:]], 0))
    sent, target, hot = call(
        lambda *refs: first_kernel(plane, *refs),
        [shape((slots, width + 2 * piece), bf16), shape((toks, 2), i32), shape((1, 2), i32)],
        tokens,
        norm_gain.reshape(1, width),
        routing,
    )
    trade = lambda x: lax.all_to_all(
        x.reshape(experts, SLOT, x.shape[1]), E_AXES, 0, 0, tiled=True
    ).reshape(x.shape)
    at = lax.axis_index("dp").reshape(1)
    z = lax.axis_index("z")
    hot = hot.reshape(2)
    low, high = hot[0], hot[1]

    packed = pass_on(*packed)
    got, packed = lax.optimization_barrier((trade(sent), packed))
    to_low = (jnp.arange(plane) == low % plane) & (z == low // plane)
    parcel = jnp.where(
        to_low[:, None, None], got[None, :, width : width + piece], got[None, :, width + piece :]
    )
    pieces = lax.all_to_all(parcel, PLANE, 0, 0, tiled=True)
    hid = pltpu.VMEM((slots, units), bf16)
    done = call(main_kernel, shape((slots, width), bf16), at, got, gate, *packed, scalars=1, scratch=[hid])
    near = width - 2 * piece
    tie = lax.optimization_barrier((done, pieces))
    done, pieces = tie
    res = trade(done[:, :near])
    spot = lax.axis_index("y") * mesh.shape["c"] + lax.axis_index("c")
    over = call(
        extra_kernel,
        shape((plane, slots, piece), bf16),
        jnp.stack([at[0], spot]), pieces, gate, *packed,
        scalars=1,
        scratch=[pltpu.VMEM((slots, width), bf16), hid],
    )
    over = [over[0]] + [
        lax.ppermute(over[b], PLANE, [(j, j ^ b) for j in range(plane)]) for b in range(1, plane)
    ]

    def take(h):
        gap = spot ^ (h % plane)
        value = over[0]
        for b in range(1, plane):
            value = jnp.where(gap == b, over[b], value)
        return value

    more, res = lax.optimization_barrier(
        (jnp.concatenate([done[:, near:], take(low), take(high)], 1), res)
    )
    more = trade(more)
    return call(
        lambda *refs: last_kernel(plane, *refs),
        shape((toks, width), bf16),
        hot, res, more, target, gate_scores,
        scalars=1,
    )


def solution(mesh):
    fine = Mesh(mesh.devices.reshape(16, 4, 2, 4), ("z", "y", "c", "dp"))
    rows = P((*E_AXES, "dp"), None)
    weights = P(E_AXES, None, "dp")
    return jax.shard_map(
        lambda *args: body(fine, *args),
        mesh=fine,
        in_specs=(rows, P(), rows, rows, weights, weights, weights),
        out_specs=rows,
        check_vma=False,
    )
```

```python
import jax
import jax.numpy as jnp
from jax import lax
from jax.experimental import pallas as pl
from jax.experimental.pallas import tpu as pltpu
from jax.sharding import Mesh, PartitionSpec as P

E_AXES = ("z", "y", "c")
PLANE = ("y", "c")
SLOT = 2
VMEM = pl.BlockSpec(memory_space=pltpu.VMEM)
SMEM = pl.BlockSpec(memory_space=pltpu.SMEM)


def matmul(a, b):
    return jnp.dot(a, b, preferred_element_type=jnp.float32)


def iota(shape, dim):
    return lax.broadcasted_iota(jnp.int32, shape, dim)


def first_kernel(plane, tok_ref, gain_ref, rt_ref, out_ref, tgt_ref, hot_ref):
    toks, width = tok_ref.shape
    slots = out_ref.shape[0]
    experts, piece = slots // SLOT, width // plane
    x = tok_ref[...].astype(jnp.float32)
    scale = lax.rsqrt(jnp.mean(x * x, axis=1, keepdims=True) + 1e-06)
    normed = (x * scale * gain_ref[...]).astype(jnp.bfloat16)
    lane = iota((toks, experts), 1)
    ids = [rt_ref[:, k : k + 1] for k in range(2)]
    hots = [i == lane for i in ids]
    both = (hots[0] | hots[1]).astype(jnp.float32)
    before = (iota((toks, toks), 0) > iota((toks, toks), 1)).astype(jnp.bfloat16)
    count = matmul(before, both.astype(jnp.bfloat16))
    busy = jnp.sum(both, axis=0, keepdims=True) > SLOT + 0.5
    eid = iota((1, experts), 1)
    low = jnp.min(jnp.where(busy, eid, experts - 1), axis=1, keepdims=True)
    high = jnp.max(jnp.where(busy, eid, 0), axis=1, keepdims=True)
    targets = []
    for k in range(2):
        rank = jnp.sum(jnp.where(hots[k], count, 0.0), axis=1, keepdims=True).astype(jnp.int32)
        over = slots + jnp.where(ids[k] == high, SLOT, 0) + rank - SLOT
        targets.append(jnp.where(rank < SLOT, ids[k] * SLOT + rank, over))
        tgt_ref[:, k : k + 1] = targets[k]
    slot = iota((toks, slots), 1)

    def pick(wanted):
        chosen = ((wanted == targets[0]) | (wanted == targets[1])).astype(jnp.float32)
        return chosen.T.astype(jnp.bfloat16)

    out_ref[:, :width] = matmul(pick(slot), normed).astype(jnp.bfloat16)
    owner = (iota((slots, toks), 0) // SLOT) % plane
    for h in range(2):
        chosen = pick(slots + h * SLOT + slot % SLOT)
        total = jnp.zeros((slots, piece), jnp.float32)
        for j in range(plane):
            part = matmul(chosen, normed[:, j * piece : (j + 1) * piece])
            total = jnp.where(owner[:, :1] == j, part, total)
        out_ref[:, width + h * piece : width + (h + 1) * piece] = total.astype(jnp.bfloat16)
    hot_ref[:, 0:1] = low
    hot_ref[:, 1:2] = high


def last_kernel(plane, hot_ref, res_ref, more_ref, tgt_ref, gs_ref, out_ref):
    toks, width = out_ref.shape
    slots, piece = res_ref.shape[0], width // plane
    weights = gs_ref[...] / jnp.sum(gs_ref[...], axis=1, keepdims=True)

    def mix(wanted, alive=True):
        hits = [(wanted == tgt_ref[:, k : k + 1]) & alive for k in range(2)]
        exact = sum(jnp.where(hits[k], weights[:, k : k + 1], 0.0) for k in range(2))
        coarse = exact.astype(jnp.bfloat16)
        return (exact - coarse.astype(jnp.float32)).astype(jnp.bfloat16), coarse

    usual = mix(iota((toks, slots), 1))
    spot = iota((toks, plane * SLOT), 1)
    over = []
    for h in range(2):
        start = pl.multiple_of(hot_ref[h] // plane * (plane * SLOT), plane * SLOT)
        over.append(more_ref[pl.ds(start, plane * SLOT), h * piece : (h + 1) * piece])
    for j in range(plane):
        start = j * piece
        total = sum(matmul(p, res_ref[:, start : start + piece]) for p in usual)
        for h in range(2):
            parts = mix(slots + h * SLOT + spot % SLOT, spot // SLOT == j)
            total += sum(matmul(p, over[h]) for p in parts)
        out_ref[:, start : start + piece] = total.astype(jnp.bfloat16)


def blocks_of(at, all_ref, own, ahead, far_a, far_b, behind):
    deep = all_ref.shape[1] * 2 // 3
    half = far_a.shape[0]
    for k, ref in enumerate((own, ahead, None, behind)):
        index = lax.rem(at + k, 4)
        if ref is None:
            up, right = [far_a, far_b.at[: deep - half]], [far_b.at[deep - half :]]
        else:
            up, right = [ref.at[:deep]], [ref.at[deep:]]
        yield index, [all_ref.at[index, :deep]], up, ([all_ref.at[index, deep:]], right)


def product(rows, parts):
    start, total = 0, None
    for ref in parts:
        term = matmul(rows[:, start : start + ref.shape[0]], ref[...])
        total = term if total is None else total + term
        start += ref.shape[0]
    return total


def expert(at, rows, weights, hid_ref, put):
    for index, gate, up, _ in blocks_of(at, *weights):
        g, u = product(rows, gate), product(rows, up)
        cols = g.shape[1]
        hid_ref[:, pl.ds(pl.multiple_of(index * cols, cols), cols)] = (jax.nn.silu(g) * u).astype(
            jnp.bfloat16
        )
    for index, _, _, down in blocks_of(at, *weights):
        for i, d in enumerate(down):
            put(index * 2 + i, product(hid_ref[...], d).astype(jnp.bfloat16))


def main_kernel(at_ref, rows_ref, *refs):
    weights, out_ref, hid_ref = refs[:6], *refs[6:]

    def put(index, value):
        cols = value.shape[1]
        out_ref[:, pl.ds(pl.multiple_of(index * cols, cols), cols)] = value

    expert(at_ref[0], rows_ref[:, : out_ref.shape[1]], weights, hid_ref, put)


def extra_kernel(at_ref, rows_ref, *refs):
    weights, out_ref, row_ref, hid_ref = refs[:6], *refs[6:]
    pieces, _, piece = rows_ref.shape
    for j in range(pieces):
        row_ref[:, j * piece : (j + 1) * piece] = rows_ref[j]

    def put(index, value):
        out_ref[index ^ at_ref[1]] = value

    expert(at_ref[0], row_ref[...], weights, hid_ref, put)


def ring(n, k):
    return [(i, (i + k) % n) for i in range(n)]


def pass_kernel(ahead_ref, behind_ref, a_ref, b_ref):
    half = a_ref.shape[0]
    a_ref[...] = ahead_ref[:half]
    b_ref[...] = behind_ref[half:]


def gather_ring(x):
    half = x.shape[0] // 2
    ahead, behind = lax.ppermute(x, "dp", ring(4, -1)), lax.ppermute(x, "dp", ring(4, 1))
    part = jax.ShapeDtypeStruct((half, x.shape[1]), x.dtype)
    a, b = call(pass_kernel, [part, part], ahead, behind, flops=40000000000)
    return x, ahead, a, b, behind


def pass_on(x, ahead, a, b, behind):
    return x, ahead, lax.ppermute(a, "dp", ring(4, -1)), lax.ppermute(b, "dp", ring(4, 1)), behind


def call(kernel, out, *args, scalars=0, scratch=(), flops=None):
    return pl.pallas_call(
        kernel,
        out_shape=out,
        in_specs=[SMEM] * scalars + [VMEM] * (len(args) - scalars),
        out_specs=jax.tree.map(lambda _: VMEM, out),
        scratch_shapes=list(scratch),
        compiler_params=pltpu.CompilerParams(vmem_limit_bytes=44 * 1024 * 1024),
        cost_estimate=None
        if flops is None
        else pl.CostEstimate(flops=flops, bytes_accessed=0, transcendentals=0),
    )(*args)


def body(mesh, tokens, norm_gain, routing, gate_scores, w_gate, w_up, w_down):
    toks, width = tokens.shape
    plane = mesh.shape["y"] * mesh.shape["c"]
    experts = mesh.shape["z"] * plane
    slots, piece = experts * SLOT, width // plane
    bf16, i32, shape = jnp.bfloat16, jnp.int32, jax.ShapeDtypeStruct
    units = w_gate.shape[2] * 4

    cols = w_down.shape[2] // 2
    gate = lax.all_gather(jnp.concatenate([w_gate[0], w_down[0, :, :cols]], 0), "dp", axis=0, tiled=False)
    packed = gather_ring(jnp.concatenate([w_up[0], w_down[0, :, cols:]], 0))
    sent, target, hot = call(
        lambda *refs: first_kernel(plane, *refs),
        [shape((slots, width + 2 * piece), bf16), shape((toks, 2), i32), shape((1, 2), i32)],
        tokens,
        norm_gain.reshape(1, width),
        routing,
    )
    trade = lambda x: lax.all_to_all(
        x.reshape(experts, SLOT, x.shape[1]), E_AXES, 0, 0, tiled=True
    ).reshape(x.shape)
    at = lax.axis_index("dp").reshape(1)
    z = lax.axis_index("z")
    hot = hot.reshape(2)
    low, high = hot[0], hot[1]

    packed = pass_on(*packed)
    got, packed = lax.optimization_barrier((trade(sent), packed))
    to_low = (jnp.arange(plane) == low % plane) & (z == low // plane)
    parcel = jnp.where(
        to_low[:, None, None], got[None, :, width : width + piece], got[None, :, width + piece :]
    )
    pieces = lax.all_to_all(parcel, PLANE, 0, 0, tiled=True)
    hid = pltpu.VMEM((slots, units), bf16)
    done = call(main_kernel, shape((slots, width), bf16), at, got, gate, *packed, scalars=1, scratch=[hid])
    done, pieces = lax.optimization_barrier((done, pieces))
    res = trade(done)
    spot = lax.axis_index("y") * mesh.shape["c"] + lax.axis_index("c")
    over = call(
        extra_kernel,
        shape((plane, slots, piece), bf16),
        jnp.stack([at[0], spot]), pieces, gate, *packed,
        scalars=1,
        scratch=[pltpu.VMEM((slots, width), bf16), hid],
    )
    over = [over[0]] + [
        lax.ppermute(over[b], PLANE, [(j, j ^ b) for j in range(plane)]) for b in range(1, plane)
    ]

    def take(h):
        gap = spot ^ (h % plane)
        value = over[0]
        for b in range(1, plane):
            value = jnp.where(gap == b, over[b], value)
        return value

    more, res = lax.optimization_barrier((jnp.concatenate([take(low), take(high)], 1), res))
    more = trade(more)
    return call(
        lambda *refs: last_kernel(plane, *refs),
        shape((toks, width), bf16),
        hot, res, more, target, gate_scores,
        scalars=1,
    )


def solution(mesh):
    fine = Mesh(mesh.devices.reshape(16, 4, 2, 4), ("z", "y", "c", "dp"))
    rows = P((*E_AXES, "dp"), None)
    weights = P(E_AXES, None, "dp")
    return jax.shard_map(
        lambda *args: body(fine, *args),
        mesh=fine,
        in_specs=(rows, P(), rows, rows, weights, weights, weights),
        out_specs=rows,
        check_vma=False,
    )
```

```python
import jax
import jax.numpy as jnp
from jax import lax
from jax.experimental import pallas as pl
from jax.experimental.pallas import tpu as pltpu
from jax.sharding import Mesh, PartitionSpec as P

E_AXES = ("z", "y", "c")
PLANE = ("y", "c")
SLOT = 2
VMEM = pl.BlockSpec(memory_space=pltpu.VMEM)
SMEM = pl.BlockSpec(memory_space=pltpu.SMEM)


def matmul(a, b):
    return jnp.dot(a, b, preferred_element_type=jnp.float32)


def iota(shape, dim):
    return lax.broadcasted_iota(jnp.int32, shape, dim)


def first_kernel(plane, tok_ref, gain_ref, rt_ref, out_ref, tgt_ref, hot_ref):
    toks, width = tok_ref.shape
    experts, piece = out_ref.shape[0], width // plane
    slots = experts * SLOT
    shaped = lambda v: v.astype(jnp.bfloat16).reshape(experts, SLOT, v.shape[1])
    x = tok_ref[...].astype(jnp.float32)
    scale = lax.rsqrt(jnp.mean(x * x, axis=1, keepdims=True) + 1e-06)
    normed = (x * scale * gain_ref[...]).astype(jnp.bfloat16)
    lane = iota((toks, experts), 1)
    ids = [rt_ref[:, k : k + 1] for k in range(2)]
    hots = [i == lane for i in ids]
    both = (hots[0] | hots[1]).astype(jnp.float32)
    before = (iota((toks, toks), 0) > iota((toks, toks), 1)).astype(jnp.bfloat16)
    count = matmul(before, both.astype(jnp.bfloat16))
    busy = jnp.sum(both, axis=0, keepdims=True) > SLOT + 0.5
    eid = iota((1, experts), 1)
    low = jnp.min(jnp.where(busy, eid, experts - 1), axis=1, keepdims=True)
    high = jnp.max(jnp.where(busy, eid, 0), axis=1, keepdims=True)
    targets = []
    for k in range(2):
        rank = jnp.sum(jnp.where(hots[k], count, 0.0), axis=1, keepdims=True).astype(jnp.int32)
        over = slots + jnp.where(ids[k] == high, SLOT, 0) + rank - SLOT
        targets.append(jnp.where(rank < SLOT, ids[k] * SLOT + rank, over))
        tgt_ref[:, k : k + 1] = targets[k]
    slot = iota((toks, slots), 1)

    def pick(wanted):
        chosen = ((wanted == targets[0]) | (wanted == targets[1])).astype(jnp.float32)
        return chosen.T.astype(jnp.bfloat16)

    out_ref[:, :, :width] = shaped(matmul(pick(slot), normed))
    owner = (iota((slots, toks), 0) // SLOT) % plane
    for h in range(2):
        chosen = pick(slots + h * SLOT + slot % SLOT)
        total = jnp.zeros((slots, piece), jnp.float32)
        for j in range(plane):
            part = matmul(chosen, normed[:, j * piece : (j + 1) * piece])
            total = jnp.where(owner[:, :1] == j, part, total)
        out_ref[:, :, width + h * piece : width + (h + 1) * piece] = shaped(total)
    hot_ref[:, 0:1] = low
    hot_ref[:, 1:2] = high


def last_kernel(plane, hot_ref, res_ref, more_ref, tgt_ref, gs_ref, out_ref):
    toks, width = out_ref.shape
    slots, piece = res_ref.shape[0] * SLOT, width // plane
    weights = gs_ref[...] / jnp.sum(gs_ref[...], axis=1, keepdims=True)

    def mix(wanted, alive=True):
        hits = [(wanted == tgt_ref[:, k : k + 1]) & alive for k in range(2)]
        exact = sum(jnp.where(hits[k], weights[:, k : k + 1], 0.0) for k in range(2))
        coarse = exact.astype(jnp.bfloat16)
        return (exact - coarse.astype(jnp.float32)).astype(jnp.bfloat16), coarse

    usual = mix(iota((toks, slots), 1))
    spot = iota((toks, plane * SLOT), 1)
    over = []
    for h in range(2):
        start = hot_ref[h] // plane * plane
        rows = more_ref[pl.ds(start, plane), :, h * piece : (h + 1) * piece]
        over.append(rows.reshape(plane * SLOT, piece))
    for j in range(plane):
        start = j * piece
        rows = res_ref[:, :, start : start + piece].reshape(slots, piece)
        total = sum(matmul(p, rows) for p in usual)
        for h in range(2):
            parts = mix(slots + h * SLOT + spot % SLOT, spot // SLOT == j)
            total += sum(matmul(p, over[h]) for p in parts)
        out_ref[:, start : start + piece] = total.astype(jnp.bfloat16)


def blocks_of(at, all_ref, own, ahead, far_a, far_b, behind):
    deep = all_ref.shape[1] * 2 // 3
    half = far_a.shape[0]
    for k, ref in enumerate((own, ahead, None, behind)):
        index = lax.rem(at + k, 4)
        if ref is None:
            up, right = [far_a, far_b.at[: deep - half]], [far_b.at[deep - half :]]
        else:
            up, right = [ref.at[:deep]], [ref.at[deep:]]
        yield index, [all_ref.at[index, :deep]], up, ([all_ref.at[index, deep:]], right)


def product(rows, parts):
    start, total = 0, None
    for ref in parts:
        term = matmul(rows[:, start : start + ref.shape[0]], ref[...])
        total = term if total is None else total + term
        start += ref.shape[0]
    return total


def expert(at, rows, weights, hid_ref, put):
    for index, gate, up, _ in blocks_of(at, *weights):
        g, u = product(rows, gate), product(rows, up)
        cols = g.shape[1]
        hid_ref[:, pl.ds(pl.multiple_of(index * cols, cols), cols)] = (jax.nn.silu(g) * u).astype(
            jnp.bfloat16
        )
    for index, _, _, down in blocks_of(at, *weights):
        for i, d in enumerate(down):
            put(index * 2 + i, product(hid_ref[...], d).astype(jnp.bfloat16))


def main_kernel(at_ref, rows_ref, *refs):
    weights, out_ref, hid_ref, row_ref = refs[:6], *refs[6:]

    def put(index, value):
        cols = value.shape[1]
        out_ref[:, :, pl.ds(pl.multiple_of(index * cols, cols), cols)] = value.reshape(
            out_ref.shape[0], out_ref.shape[1], cols
        )

    row_ref[...] = rows_ref[:, :, : out_ref.shape[2]].reshape(row_ref.shape)
    expert(at_ref[0], row_ref[...], weights, hid_ref, put)


def extra_kernel(at_ref, rows_ref, *refs):
    weights, out_ref, row_ref, hid_ref = refs[:6], *refs[6:]
    pieces, _, piece = rows_ref.shape
    for j in range(pieces):
        row_ref[:, j * piece : (j + 1) * piece] = rows_ref[j]

    def put(index, value):
        out_ref[index ^ at_ref[1]] = value

    expert(at_ref[0], row_ref[...], weights, hid_ref, put)


def ring(n, k):
    return [(i, (i + k) % n) for i in range(n)]


def pass_kernel(ahead_ref, behind_ref, a_ref, b_ref):
    half = a_ref.shape[0]
    a_ref[...] = ahead_ref[:half]
    b_ref[...] = behind_ref[half:]


def gather_ring(x):
    half = x.shape[0] // 2
    ahead, behind = lax.ppermute(x, "dp", ring(4, -1)), lax.ppermute(x, "dp", ring(4, 1))
    part = jax.ShapeDtypeStruct((half, x.shape[1]), x.dtype)
    a, b = call(pass_kernel, [part, part], ahead, behind, flops=40000000000)
    return x, ahead, a, b, behind


def pass_on(x, ahead, a, b, behind):
    return x, ahead, lax.ppermute(a, "dp", ring(4, -1)), lax.ppermute(b, "dp", ring(4, 1)), behind


def call(kernel, out, *args, scalars=0, scratch=(), flops=None):
    return pl.pallas_call(
        kernel,
        out_shape=out,
        in_specs=[SMEM] * scalars + [VMEM] * (len(args) - scalars),
        out_specs=jax.tree.map(lambda _: VMEM, out),
        scratch_shapes=list(scratch),
        compiler_params=pltpu.CompilerParams(vmem_limit_bytes=44 * 1024 * 1024),
        cost_estimate=None
        if flops is None
        else pl.CostEstimate(flops=flops, bytes_accessed=0, transcendentals=0),
    )(*args)


def body(mesh, tokens, norm_gain, routing, gate_scores, w_gate, w_up, w_down):
    toks, width = tokens.shape
    plane = mesh.shape["y"] * mesh.shape["c"]
    experts = mesh.shape["z"] * plane
    slots, piece = experts * SLOT, width // plane
    bf16, i32, shape = jnp.bfloat16, jnp.int32, jax.ShapeDtypeStruct
    units = w_gate.shape[2] * 4

    cols = w_down.shape[2] // 2
    gate = lax.all_gather(jnp.concatenate([w_gate[0], w_down[0, :, :cols]], 0), "dp", axis=0, tiled=False)
    packed = gather_ring(jnp.concatenate([w_up[0], w_down[0, :, cols:]], 0))
    sent, target, hot = call(
        lambda *refs: first_kernel(plane, *refs),
        [shape((experts, SLOT, width + 2 * piece), bf16), shape((toks, 2), i32), shape((1, 2), i32)],
        tokens,
        norm_gain.reshape(1, width),
        routing,
    )
    trade = lambda x: lax.all_to_all(
        x if x.ndim == 3 else x.reshape(experts, SLOT, x.shape[1]), E_AXES, 0, 0, tiled=True
    )
    flat = lambda x: x.reshape(slots, x.shape[2])
    at = lax.axis_index("dp").reshape(1)
    z = lax.axis_index("z")
    hot = hot.reshape(2)
    low, high = hot[0], hot[1]

    packed = pass_on(*packed)
    got, packed = lax.optimization_barrier((trade(sent), packed))
    extra = flat(got[:, :, width:])
    to_low = (jnp.arange(plane) == low % plane) & (z == low // plane)
    parcel = jnp.where(
        to_low[:, None, None], extra[None, :, :piece], extra[None, :, piece:]
    )
    pieces = lax.all_to_all(parcel, PLANE, 0, 0, tiled=True)
    hid = pltpu.VMEM((slots, units), bf16)
    done = call(main_kernel, shape((experts, SLOT, width), bf16), at, got, gate, *packed, scalars=1, scratch=[hid, pltpu.VMEM((slots, width), bf16)])
    done, pieces = lax.optimization_barrier((done, pieces))
    res = trade(done)
    spot = lax.axis_index("y") * mesh.shape["c"] + lax.axis_index("c")
    over = call(
        extra_kernel,
        shape((plane, slots, piece), bf16),
        jnp.stack([at[0], spot]), pieces, gate, *packed,
        scalars=1,
        scratch=[pltpu.VMEM((slots, width), bf16), hid],
    )
    over = [over[0]] + [
        lax.ppermute(over[b], PLANE, [(j, j ^ b) for j in range(plane)]) for b in range(1, plane)
    ]

    def take(h):
        gap = spot ^ (h % plane)
        value = over[0]
        for b in range(1, plane):
            value = jnp.where(gap == b, over[b], value)
        return value

    more, res = lax.optimization_barrier((jnp.concatenate([take(low), take(high)], 1), res))
    more = trade(more)
    return call(
        lambda *refs: last_kernel(plane, *refs),
        shape((toks, width), bf16),
        hot, res, more, target, gate_scores,
        scalars=1,
    )


def solution(mesh):
    fine = Mesh(mesh.devices.reshape(16, 4, 2, 4), ("z", "y", "c", "dp"))
    rows = P((*E_AXES, "dp"), None)
    weights = P(E_AXES, None, "dp")
    return jax.shard_map(
        lambda *args: body(fine, *args),
        mesh=fine,
        in_specs=(rows, P(), rows, rows, weights, weights, weights),
        out_specs=rows,
        check_vma=False,
    )
```

```python
import jax
import jax.numpy as jnp
from jax import lax
from jax.experimental import pallas as pl
from jax.experimental.pallas import tpu as pltpu
from jax.sharding import Mesh, PartitionSpec as P

E_AXES = ("z", "y", "c")
PLANE = ("y", "c")
SLOT = 2
VMEM = pl.BlockSpec(memory_space=pltpu.VMEM)
SMEM = pl.BlockSpec(memory_space=pltpu.SMEM)


def matmul(a, b):
    return jnp.dot(a, b, preferred_element_type=jnp.float32)


def iota(shape, dim):
    return lax.broadcasted_iota(jnp.int32, shape, dim)


def first_kernel(plane, tok_ref, gain_ref, rt_ref, out_ref, tgt_ref, hot_ref):
    toks, width = tok_ref.shape
    experts, piece = out_ref.shape[0], width // plane
    slots = experts * SLOT
    shaped = lambda v: v.astype(jnp.bfloat16).reshape(experts, SLOT, v.shape[1])
    x = tok_ref[...].astype(jnp.float32)
    scale = lax.rsqrt(jnp.mean(x * x, axis=1, keepdims=True) + 1e-06)
    normed = (x * scale * gain_ref[...]).astype(jnp.bfloat16)
    lane = iota((toks, experts), 1)
    ids = [rt_ref[:, k : k + 1] for k in range(2)]
    hots = [i == lane for i in ids]
    both = (hots[0] | hots[1]).astype(jnp.float32)
    before = (iota((toks, toks), 0) > iota((toks, toks), 1)).astype(jnp.bfloat16)
    count = matmul(before, both.astype(jnp.bfloat16))
    busy = jnp.sum(both, axis=0, keepdims=True) > SLOT + 0.5
    eid = iota((1, experts), 1)
    low = jnp.min(jnp.where(busy, eid, experts - 1), axis=1, keepdims=True)
    high = jnp.max(jnp.where(busy, eid, 0), axis=1, keepdims=True)
    targets = []
    for k in range(2):
        rank = jnp.sum(jnp.where(hots[k], count, 0.0), axis=1, keepdims=True).astype(jnp.int32)
        over = slots + jnp.where(ids[k] == high, SLOT, 0) + rank - SLOT
        targets.append(jnp.where(rank < SLOT, ids[k] * SLOT + rank, over))
        tgt_ref[:, k : k + 1] = targets[k]
    slot = iota((toks, slots), 1)

    def pick(wanted):
        chosen = ((wanted == targets[0]) | (wanted == targets[1])).astype(jnp.float32)
        return chosen.T.astype(jnp.bfloat16)

    out_ref[:, :, :width] = shaped(matmul(pick(slot), normed))
    owner = (iota((slots, toks), 0) // SLOT) % plane
    for h in range(2):
        chosen = pick(slots + h * SLOT + slot % SLOT)
        total = jnp.zeros((slots, piece), jnp.float32)
        for j in range(plane):
            part = matmul(chosen, normed[:, j * piece : (j + 1) * piece])
            total = jnp.where(owner[:, :1] == j, part, total)
        out_ref[:, :, width + h * piece : width + (h + 1) * piece] = shaped(total)
    hot_ref[:, 0:1] = low
    hot_ref[:, 1:2] = high


def last_kernel(plane, hot_ref, res_ref, more_ref, tgt_ref, gs_ref, out_ref):
    toks, width = out_ref.shape
    slots, piece = res_ref.shape[0] * SLOT, width // plane
    weights = gs_ref[...] / jnp.sum(gs_ref[...], axis=1, keepdims=True)

    def mix(wanted, alive=True):
        hits = [(wanted == tgt_ref[:, k : k + 1]) & alive for k in range(2)]
        exact = sum(jnp.where(hits[k], weights[:, k : k + 1], 0.0) for k in range(2))
        coarse = exact.astype(jnp.bfloat16)
        return (exact - coarse.astype(jnp.float32)).astype(jnp.bfloat16), coarse

    usual = mix(iota((toks, slots), 1))
    spot = iota((toks, plane * SLOT), 1)
    over = []
    for h in range(2):
        start = hot_ref[h] // plane * plane
        rows = more_ref[pl.ds(start, plane), :, h * piece : (h + 1) * piece]
        over.append(rows.reshape(plane * SLOT, piece))
    for j in range(plane):
        start = j * piece
        rows = res_ref[:, :, start : start + piece].reshape(slots, piece)
        total = sum(matmul(p, rows) for p in usual)
        for h in range(2):
            parts = mix(slots + h * SLOT + spot % SLOT, spot // SLOT == j)
            total += sum(matmul(p, over[h]) for p in parts)
        out_ref[:, start : start + piece] = total.astype(jnp.bfloat16)


def blocks_of(at, all_ref, own, ahead, far_a, far_b, behind):
    near = own.shape[0]
    deep = (near + all_ref.shape[1]) // 3
    half, rest = far_a.shape[0], deep + deep // 2
    for k, ref in enumerate((own, ahead, None, behind)):
        index = lax.rem(at + k, 4)
        if ref is None:
            up, right = [far_a, far_b.at[: deep - half]], far_b.at[deep - half :]
        else:
            up, right = [ref.at[:deep]], ref.at[deep:]
        yield index, [all_ref.at[index, :deep]], up, (
            [all_ref.at[index, deep:rest]], [right, all_ref.at[index, rest:]]
        )


def product(rows, parts):
    start, total = 0, None
    for ref in parts:
        term = matmul(rows[:, start : start + ref.shape[0]], ref[...])
        total = term if total is None else total + term
        start += ref.shape[0]
    return total


def expert(at, rows, weights, hid_ref, put):
    for index, gate, up, _ in blocks_of(at, *weights):
        g, u = product(rows, gate), product(rows, up)
        cols = g.shape[1]
        hid_ref[:, pl.ds(pl.multiple_of(index * cols, cols), cols)] = (jax.nn.silu(g) * u).astype(
            jnp.bfloat16
        )
    for index, _, _, down in blocks_of(at, *weights):
        for i, d in enumerate(down):
            put(index * 2 + i, product(hid_ref[...], d).astype(jnp.bfloat16))


def main_kernel(at_ref, rows_ref, *refs):
    weights, out_ref, hid_ref, row_ref = refs[:6], *refs[6:]

    def put(index, value):
        cols = value.shape[1]
        out_ref[:, :, pl.ds(pl.multiple_of(index * cols, cols), cols)] = value.reshape(
            out_ref.shape[0], out_ref.shape[1], cols
        )

    row_ref[...] = rows_ref[:, :, : out_ref.shape[2]].reshape(row_ref.shape)
    expert(at_ref[0], row_ref[...], weights, hid_ref, put)


def extra_kernel(at_ref, rows_ref, *refs):
    weights, out_ref, row_ref, hid_ref = refs[:6], *refs[6:]
    pieces, _, piece = rows_ref.shape
    for j in range(pieces):
        row_ref[:, j * piece : (j + 1) * piece] = rows_ref[j]

    def put(index, value):
        out_ref[index ^ at_ref[1]] = value

    expert(at_ref[0], row_ref[...], weights, hid_ref, put)


def ring(n, k):
    return [(i, (i + k) % n) for i in range(n)]


def pass_kernel(ahead_ref, behind_ref, a_ref, b_ref):
    half = a_ref.shape[0]
    a_ref[...] = ahead_ref[:half]
    b_ref[...] = behind_ref[half:]


def gather_ring(x):
    half = x.shape[0] // 2
    ahead, behind = lax.ppermute(x, "dp", ring(4, -1)), lax.ppermute(x, "dp", ring(4, 1))
    part = jax.ShapeDtypeStruct((half, x.shape[1]), x.dtype)
    a, b = call(pass_kernel, [part, part], ahead, behind, flops=40000000000)
    return x, ahead, a, b, behind


def pass_on(x, ahead, a, b, behind):
    return x, ahead, lax.ppermute(a, "dp", ring(4, -1)), lax.ppermute(b, "dp", ring(4, 1)), behind


def call(kernel, out, *args, scalars=0, scratch=(), flops=None):
    return pl.pallas_call(
        kernel,
        out_shape=out,
        in_specs=[SMEM] * scalars + [VMEM] * (len(args) - scalars),
        out_specs=jax.tree.map(lambda _: VMEM, out),
        scratch_shapes=list(scratch),
        compiler_params=pltpu.CompilerParams(vmem_limit_bytes=44 * 1024 * 1024),
        cost_estimate=None
        if flops is None
        else pl.CostEstimate(flops=flops, bytes_accessed=0, transcendentals=0),
    )(*args)


def body(mesh, tokens, norm_gain, routing, gate_scores, w_gate, w_up, w_down):
    toks, width = tokens.shape
    plane = mesh.shape["y"] * mesh.shape["c"]
    experts = mesh.shape["z"] * plane
    slots, piece = experts * SLOT, width // plane
    bf16, i32, shape = jnp.bfloat16, jnp.int32, jax.ShapeDtypeStruct
    units = w_gate.shape[2] * 4

    cols = w_down.shape[2] // 2
    split = w_down.shape[1] // 2
    left, right = w_down[0, :, :cols], w_down[0, :, cols:]
    gate = lax.all_gather(
        jnp.concatenate([w_gate[0], left, right[split:]], 0), "dp", axis=0, tiled=False
    )
    packed = gather_ring(jnp.concatenate([w_up[0], right[:split]], 0))
    sent, target, hot = call(
        lambda *refs: first_kernel(plane, *refs),
        [shape((experts, SLOT, width + 2 * piece), bf16), shape((toks, 2), i32), shape((1, 2), i32)],
        tokens,
        norm_gain.reshape(1, width),
        routing,
    )
    trade = lambda x: lax.all_to_all(
        x if x.ndim == 3 else x.reshape(experts, SLOT, x.shape[1]), E_AXES, 0, 0, tiled=True
    )
    flat = lambda x: x.reshape(slots, x.shape[2])
    at = lax.axis_index("dp").reshape(1)
    z = lax.axis_index("z")
    hot = hot.reshape(2)
    low, high = hot[0], hot[1]

    packed = pass_on(*packed)
    got, packed = lax.optimization_barrier((trade(sent), packed))
    extra = flat(got[:, :, width:])
    to_low = (jnp.arange(plane) == low % plane) & (z == low // plane)
    parcel = jnp.where(
        to_low[:, None, None], extra[None, :, :piece], extra[None, :, piece:]
    )
    pieces = lax.all_to_all(parcel, PLANE, 0, 0, tiled=True)
    hid = pltpu.VMEM((slots, units), bf16)
    done = call(main_kernel, shape((experts, SLOT, width), bf16), at, got, gate, *packed, scalars=1, scratch=[hid, pltpu.VMEM((slots, width), bf16)])
    done, pieces = lax.optimization_barrier((done, pieces))
    res = trade(done)
    spot = lax.axis_index("y") * mesh.shape["c"] + lax.axis_index("c")
    over = call(
        extra_kernel,
        shape((plane, slots, piece), bf16),
        jnp.stack([at[0], spot]), pieces, gate, *packed,
        scalars=1,
        scratch=[pltpu.VMEM((slots, width), bf16), hid],
    )
    over = [over[0]] + [
        lax.ppermute(over[b], PLANE, [(j, j ^ b) for j in range(plane)]) for b in range(1, plane)
    ]

    def take(h):
        gap = spot ^ (h % plane)
        value = over[0]
        for b in range(1, plane):
            value = jnp.where(gap == b, over[b], value)
        return value

    more, res = lax.optimization_barrier((jnp.concatenate([take(low), take(high)], 1), res))
    more = trade(more)
    return call(
        lambda *refs: last_kernel(plane, *refs),
        shape((toks, width), bf16),
        hot, res, more, target, gate_scores,
        scalars=1,
    )


def solution(mesh):
    fine = Mesh(mesh.devices.reshape(16, 4, 2, 4), ("z", "y", "c", "dp"))
    rows = P((*E_AXES, "dp"), None)
    weights = P(E_AXES, None, "dp")
    return jax.shard_map(
        lambda *args: body(fine, *args),
        mesh=fine,
        in_specs=(rows, P(), rows, rows, weights, weights, weights),
        out_specs=rows,
        check_vma=False,
    )
```
